32 devices in a mesh: section: 4 (over y, core), ctx: 4 (over z), dp: 2 (over x).
Axes of the slice: x: 2, y: 2, z: 4, core: 2. Of those that a mesh axis runs over, the one named last changes fastest.
Arguments:
- q_in: bfloat16 [2, 4, 512, 2048], P('dp', 'section', 'ctx'), may hold values from -6 to 6
- key_input: bfloat16 [2, 4, 512, 512], P('dp', 'section', 'ctx'), may hold values from -6 to 6
- value_input: bfloat16 [2, 4, 512, 512], P('dp', 'section', 'ctx'), may hold values from -6 to 6
- output_saved: bfloat16 [2, 4, 512, 2048], P('dp', 'section', 'ctx'), may hold values from -6 to 6
- output_gradient: bfloat16 [2, 4, 512, 2048], P('dp', 'section', 'ctx'), may hold values from -6 to 6
- lse: float32 [2, 4, 16, 512], P('dp', 'section', None, 'ctx'), may hold values from 2 to 5
- bias_q: bfloat16 [4, 2048], P('section'), may hold values from -3 to 3
- key_bias: bfloat16 [4, 512], P('section'), may hold values from -3 to 3
- value_bias: bfloat16 [4, 512], P('section'), may hold values from -3 to 3
Outputs:
- recv_q: bfloat16 [2, 4, 512, 2048], P('dp', 'section', 'ctx')
- recv_k: bfloat16 [2, 4, 512, 512], P('dp', 'section', 'ctx')
- recv_v: bfloat16 [2, 4, 512, 512], P('dp', 'section', 'ctx')
- grad_bq: float32 [4, 2048], P('section')
- grad_bk: float32 [4, 512], P('section')
- grad_bv: float32 [4, 512], P('section')
The draws below stay inside these ranges and needn't reach their ends.
All inputs are finite; a program needn't handle non-finite values.
Results may differ from the reference program's by a relative error of at most 0.0035.
The reference program's roundings to bfloat16 on the way count: a program that leaves them out, or rounds other values in their place, can miss the bound.
Values may be sent and summed in bfloat16 or wider, within the bound.
A program may use at most 64 MiB of HBM per device.

```python
import math
import jax
import jax.numpy as jnp
from jax import lax

QUERY_HEADS = 16
KEY_VALUE_HEADS = 4
HEAD_SIZE = 128
TOK_DEV = 128
BATCH_TOKENS = 512
RELAY_SECTIONS = 4
DATA_REPLICAS = 2
N_SECTION = 4
N_CTX = 4
N_DP = 2


def shard_levels(own_key, shape, split, least, largest):
    level = 1.0
    for dim, blocks in split:
        heights = jax.random.uniform(jax.random.fold_in(jax.random.fold_in(own_key, 6), dim), (blocks,), jnp.float32, least / len(split), largest / len(split))
        level = level * jnp.repeat(jnp.exp(heights), shape[dim] // blocks).reshape((-1,) + (1,) * (len(shape) - 1 - dim))
    return level


def scatter_about(own_key, extent, deviation, bound, split=(), kind=jnp.bfloat16):
    values = deviation * jax.random.normal(own_key, extent, jnp.float32)
    if split:
        values = values * shard_levels(own_key, extent, split, -0.22, 0.18)
    return jnp.clip(values, -bound, bound).astype(kind)


def setup_inputs(seed: int = 0) -> dict:
    splits = jax.random.split(jax.random.key(seed), 10)
    return {
        "q_in": scatter_about(splits[0], (DATA_REPLICAS, RELAY_SECTIONS, BATCH_TOKENS, QUERY_HEADS * HEAD_SIZE), 1.0, 6.0, ((0, 2), (1, 4), (2, 4))),
        "key_input": scatter_about(splits[1], (DATA_REPLICAS, RELAY_SECTIONS, BATCH_TOKENS, KEY_VALUE_HEADS * HEAD_SIZE), 1.0, 6.0, ((0, 2), (1, 4), (2, 4))),
        "value_input": scatter_about(splits[2], (DATA_REPLICAS, RELAY_SECTIONS, BATCH_TOKENS, KEY_VALUE_HEADS * HEAD_SIZE), 1.0, 6.0, ((0, 2), (1, 4), (2, 4))),
        "output_saved": scatter_about(splits[3], (DATA_REPLICAS, RELAY_SECTIONS, BATCH_TOKENS, QUERY_HEADS * HEAD_SIZE), 1.0, 6.0, ((0, 2), (1, 4), (2, 4))),
        "output_gradient": scatter_about(splits[4], (DATA_REPLICAS, RELAY_SECTIONS, BATCH_TOKENS, QUERY_HEADS * HEAD_SIZE), 1.0, 6.0, ((0, 2), (1, 4), (2, 4))),
        "lse": jnp.clip(2.0 + 3.0 * jax.random.uniform(splits[5], (DATA_REPLICAS, RELAY_SECTIONS, QUERY_HEADS, BATCH_TOKENS), jnp.float32) ** shard_levels(splits[5], (DATA_REPLICAS, RELAY_SECTIONS, QUERY_HEADS, BATCH_TOKENS), ((0, 2), (1, 4), (3, 4)), -0.2, 0.2), 2.0, 5.0),
        "bias_q": scatter_about(splits[6], (RELAY_SECTIONS, QUERY_HEADS * HEAD_SIZE), 0.5, 3.0, ((0, 4),)),
        "key_bias": scatter_about(splits[7], (RELAY_SECTIONS, KEY_VALUE_HEADS * HEAD_SIZE), 0.5, 3.0, ((0, 4),)),
        "value_bias": scatter_about(splits[8], (RELAY_SECTIONS, KEY_VALUE_HEADS * HEAD_SIZE), 0.5, 3.0, ((0, 4),)),
    }


def token_position(rows, block_rows, block_count):
    half_rows = block_rows // 2
    owner = rows // block_rows
    local = rows % block_rows
    early = owner * half_rows + local
    late = (2 * block_count - 1 - owner) * half_rows + local - half_rows
    return jnp.where(local < half_rows, early, late).astype(jnp.int32)

def backward_item(operands):
    q_in, key_input, value_input, output_saved, output_gradient, lse, bias_q, key_bias, value_bias = operands
    token_rows = q_in.shape[0]
    query_groups = QUERY_HEADS // KEY_VALUE_HEADS
    att_scale = 1.0 / math.sqrt(HEAD_SIZE)
    query_lowered = (q_in.astype(jnp.float32) + bias_q.astype(jnp.float32)).astype(jnp.bfloat16)
    key_lowered = (key_input.astype(jnp.float32) + key_bias.astype(jnp.float32)).astype(jnp.bfloat16)
    value_lowered = (value_input.astype(jnp.float32) + value_bias.astype(jnp.float32)).astype(jnp.bfloat16)
    query_grouped = query_lowered.astype(jnp.float32).reshape(token_rows, KEY_VALUE_HEADS, query_groups, HEAD_SIZE)
    key_row_list = key_lowered.astype(jnp.float32).reshape(token_rows, KEY_VALUE_HEADS, HEAD_SIZE)
    value_row_list = value_lowered.astype(jnp.float32).reshape(token_rows, KEY_VALUE_HEADS, HEAD_SIZE)
    output_gradient_grouped = output_gradient.astype(jnp.float32).reshape(token_rows, KEY_VALUE_HEADS, query_groups, HEAD_SIZE)
    output_grouped = output_saved.astype(jnp.float32).reshape(token_rows, KEY_VALUE_HEADS, query_groups, HEAD_SIZE)
    row_delta = jnp.transpose(lax.optimization_barrier(jnp.sum(output_gradient_grouped * output_grouped, axis=-1)), (1, 2, 0))
    scores = jnp.einsum('ikgd,jkd->kgij', query_grouped, key_row_list) * att_scale
    positions = token_position(jnp.arange(token_rows, dtype=jnp.int32), TOK_DEV, N_CTX)
    causal = positions[None, :] <= positions[:, None]
    logsumexp_grouped = lse.reshape(KEY_VALUE_HEADS, query_groups, token_rows)
    soft_prob = jnp.where(causal, jnp.exp(scores - logsumexp_grouped[..., None]), 0.0)
    grad_prob = jnp.einsum('ikgd,jkd->kgij', output_gradient_grouped, value_row_list)
    grad_score = soft_prob * (grad_prob - row_delta[..., None])
    prob_low = lax.optimization_barrier(soft_prob.astype(jnp.bfloat16)).astype(jnp.float32)
    score_low = lax.optimization_barrier(grad_score.astype(jnp.bfloat16)).astype(jnp.float32)
    grad_q = jnp.einsum('kgij,jkd->ikgd', score_low, key_row_list) * att_scale
    key_gradient = jnp.einsum('kgij,ikgd->jkd', score_low, query_grouped) * att_scale
    value_gradient = jnp.einsum('kgij,ikgd->jkd', prob_low, output_gradient_grouped)
    grad_q = grad_q.reshape(token_rows, QUERY_HEADS * HEAD_SIZE)
    key_gradient = key_gradient.reshape(token_rows, KEY_VALUE_HEADS * HEAD_SIZE)
    value_gradient = value_gradient.reshape(token_rows, KEY_VALUE_HEADS * HEAD_SIZE)
    return (grad_q.astype(jnp.bfloat16), key_gradient.astype(jnp.bfloat16), value_gradient.astype(jnp.bfloat16), lax.optimization_barrier(jnp.sum(grad_q, axis=0)), lax.optimization_barrier(jnp.sum(key_gradient, axis=0)), lax.optimization_barrier(jnp.sum(value_gradient, axis=0)))

def reference(q_in, key_input, value_input, output_saved, output_gradient, lse, bias_q, key_bias, value_bias):
    entries = N_DP * N_SECTION

    def flatten_items(array):
        return array.reshape((entries,) + array.shape[2:])

    def section_bias(bias):
        return jnp.broadcast_to(bias[None], (N_DP,) + bias.shape).reshape((entries, bias.shape[1]))
    results = lax.map(backward_item, (flatten_items(q_in), flatten_items(key_input), flatten_items(value_input), flatten_items(output_saved), flatten_items(output_gradient), flatten_items(lse), section_bias(bias_q), section_bias(key_bias), section_bias(value_bias)))
    grad_q, key_gradient, value_gradient, sum_q, sum_k, sum_v = results

    def unflatten(array):
        return array.reshape((N_DP, N_SECTION) + array.shape[1:])

    def passed_back(array):
        whole = unflatten(array)
        return jnp.concatenate([whole[:, 1:], jnp.zeros_like(whole[:, :1])], axis=1)
    return (passed_back(grad_q), passed_back(key_gradient), passed_back(value_gradient), lax.optimization_barrier(jnp.sum(unflatten(sum_q), axis=0)), lax.optimization_barrier(jnp.sum(unflatten(sum_k), axis=0)), lax.optimization_barrier(jnp.sum(unflatten(sum_v), axis=0)))
```

```python
import functools
import math

import jax
import jax.numpy as jnp
from jax import lax
from jax.experimental import pallas as pl
from jax.experimental.pallas import tpu as pltpu
from jax.sharding import PartitionSpec as P

QUERY_HEADS = 16
KEY_VALUE_HEADS = 4
HEAD_SIZE = 128
GROUP = QUERY_HEADS // KEY_VALUE_HEADS
GROUP_WIDTH = GROUP * HEAD_SIZE
MESH = pl.DeviceIdType.MESH
NT = (((1,), (1,)), ((), ()))
NN = (((1,), (0,)), ((), ()))


def partner(me, step, size):
    if size == 4:
        high, low = me // 2, me % 2
        high = 1 - high if step // 2 else high
        low = 1 - low if step % 2 else low
        return 2 * high + low
    return (me + step) % size


def kernel(
    n_section,
    n_ctx,
    n_dp,
    q_ref,
    k_ref,
    v_ref,
    o_ref,
    g_ref,
    lse_ref,
    bq_ref,
    bk_ref,
    bv_ref,
    rq_ref,
    rk_ref,
    rv_ref,
    sum_q_ref,
    sum_k_ref,
    sum_v_ref,
    q_in,
    g_in,
    k_in,
    v_in,
    rows_in,
    rows_out,
    o_own,
    g_own,
    bias,
    k_all,
    v_all,
    k_turned,
    grad_k,
    grad_v,
    grad_q_turned,
    q_stack,
    g_stack,
    q_out,
    k_out,
    v_out,
    sums,
    in_send,
    in_recv,
    out_send,
    out_recv,
    sum_send,
    sum_recv,
    local_sem,
):
    tokens = q_in.shape[1]
    half = tokens // 2
    scale = 1.0 / math.sqrt(HEAD_SIZE)
    section = lax.axis_index("section")
    me = lax.axis_index("ctx")
    replica = lax.axis_index("dp")
    everyone = n_ctx * n_dp
    my_place = replica * n_ctx + me
    has_before = section > 0
    has_after = section < n_section - 1

    def ctx_device(ctx):
        return {"section": section, "ctx": ctx, "dp": replica}

    def before_device(ctx):
        return {"section": section - 1, "ctx": ctx, "dp": replica}

    def after_device(ctx):
        return {"section": section + 1, "ctx": ctx, "dp": replica}

    def place_device(place):
        return {"section": section, "ctx": place % n_ctx, "dp": place // n_ctx}

    def group_columns(ctx, width):
        return pl.ds(pl.multiple_of(ctx * width, width), width)

    def sources(ctx):
        wide, narrow = group_columns(ctx, GROUP_WIDTH), group_columns(ctx, HEAD_SIZE)
        return (
            (k_ref.at[0, 0, :, narrow], k_in),
            (v_ref.at[0, 0, :, narrow], v_in),
            (q_ref.at[0, 0, :, wide], q_in),
            (g_ref.at[0, 0, :, wide], g_in),
            (rows_out.at[ctx], rows_in),
        )

    def in_copy(item, to, slot):
        source, target = sources(to)[item]
        return pltpu.make_async_remote_copy(
            src_ref=source,
            dst_ref=target.at[slot],
            send_sem=in_send.at[to, item],
            recv_sem=in_recv.at[slot, item],
            device_id=ctx_device(to),
            device_id_type=MESH,
        )

    def own_copy(item):
        source, target = sources(me)[item]
        return pltpu.make_async_copy(source, target.at[me], local_sem.at[item])

    def out_copies(ctx, slot):
        wide, narrow = group_columns(slot, GROUP_WIDTH), group_columns(slot, HEAD_SIZE)
        return [
            pltpu.make_async_remote_copy(
                src_ref=source.at[ctx],
                dst_ref=target,
                send_sem=out_send.at[ctx, item],
                recv_sem=out_recv.at[slot, item],
                device_id=before_device(ctx),
                device_id_type=MESH,
            )
            for item, (source, target) in enumerate(
                (
                    (q_out, rq_ref.at[0, 0, :, wide]),
                    (k_out, rk_ref.at[0, 0, :, narrow]),
                    (v_out, rv_ref.at[0, 0, :, narrow]),
                )
            )
        ]

    def sum_copy(place, slot):
        return pltpu.make_async_remote_copy(
            src_ref=sums.at[my_place],
            dst_ref=sums.at[slot],
            send_sem=sum_send.at[place],
            recv_sem=sum_recv.at[slot],
            device_id=place_device(place),
            device_id_type=MESH,
        )

    o_copy = pltpu.make_async_copy(o_ref.at[0, 0], o_own, local_sem.at[4])
    g_copy = pltpu.make_async_copy(g_ref.at[0, 0], g_own, local_sem.at[5])

    barrier = pltpu.get_barrier_semaphore()
    for step in range(1, everyone):
        pl.semaphore_signal(
            barrier,
            inc=1,
            device_id=place_device((my_place + step) % everyone),
            device_id_type=MESH,
        )

    @pl.when(has_before)
    def _():
        for ctx in range(n_ctx):
            pl.semaphore_signal(barrier, inc=1, device_id=before_device(ctx), device_id_type=MESH)

    @pl.when(has_after)
    def _():
        for ctx in range(n_ctx):
            pl.semaphore_signal(barrier, inc=1, device_id=after_device(ctx), device_id_type=MESH)

    o_copy.start()
    g_copy.start()
    for item in range(4):
        own_copy(item).start()
    bias[:, :GROUP_WIDTH] = jnp.zeros((8, GROUP_WIDTH), jnp.float32)

    neighbours = jnp.where(has_before, n_ctx, 0) + jnp.where(has_after, n_ctx, 0)
    pl.semaphore_wait(barrier, everyone - 1 + neighbours)

    for items in ((0, 1), (2, 3)):
        for step in reversed(range(1, n_ctx)):
            for item in items:
                in_copy(item, partner(me, step, n_ctx), me).start()

    o_copy.wait()
    g_copy.wait()
    for group in range(KEY_VALUE_HEADS):
        lines = [lse_ref[0, 0, pl.ds(group * GROUP, GROUP), :]]
        for head in range(group * GROUP, (group + 1) * GROUP):
            columns = slice(head * HEAD_SIZE, (head + 1) * HEAD_SIZE)
            product = g_own[:, columns].astype(jnp.float32) * o_own[:, columns].astype(jnp.float32)
            lines.append(jnp.sum(product.T, axis=0, keepdims=True))
        rows_out[group] = jnp.concatenate(lines, axis=0)
    for step in reversed(range(1, n_ctx)):
        in_copy(4, partner(me, step, n_ctx), me).start()
    rows_in[me] = rows_out[me]

    for ctx in range(n_ctx):
        wide = slice(ctx * GROUP_WIDTH, (ctx + 1) * GROUP_WIDTH)
        narrow = slice(ctx * HEAD_SIZE, (ctx + 1) * HEAD_SIZE)

        @pl.when(me == ctx)
        def _():
            bias[0:1, :] = bq_ref[:, wide].astype(jnp.float32)
            bias[1:2, :HEAD_SIZE] = bk_ref[:, narrow].astype(jnp.float32)
            bias[2:3, :HEAD_SIZE] = bv_ref[:, narrow].astype(jnp.float32)

    for item in range(4):
        own_copy(item).wait()
    for step in range(1, n_ctx):
        for item in (0, 1):
            in_copy(item, partner(me, step, n_ctx), partner(me, step, n_ctx)).wait_recv()
    for ctx in range(n_ctx):
        k_low = (k_in[ctx].astype(jnp.float32) + bias[1:2, :HEAD_SIZE]).astype(jnp.bfloat16)
        k_all[ctx] = k_low
        k_turned[ctx] = k_low.astype(jnp.float32).T.astype(jnp.bfloat16)
        v_all[ctx] = (v_in[ctx].astype(jnp.float32) + bias[2:3, :HEAD_SIZE]).astype(jnp.bfloat16)
    grad_k[...] = jnp.zeros_like(grad_k)
    grad_v[...] = jnp.zeros_like(grad_v)

    def positions(block, local):
        late = (2 * n_ctx - 1 - block) * half + local - half
        return jnp.where(local < half, block * half + local, late)

    q_local = jnp.concatenate(
        [lax.broadcasted_iota(jnp.int32, (1, tokens), 1)] * GROUP, axis=1
    )
    k_local = lax.broadcasted_iota(jnp.int32, (tokens, 1), 0)
    head_sums = [jnp.zeros((1, HEAD_SIZE), jnp.float32) for _ in range(GROUP)]

    for step in range(n_ctx):
        block = partner(me, step, n_ctx)
        if step:
            for item in (2, 3, 4):
                in_copy(item, block, block).wait_recv()
        for head in range(GROUP):
            columns = slice(head * HEAD_SIZE, (head + 1) * HEAD_SIZE)
            rows = slice(head * tokens, (head + 1) * tokens)
            q_stack[rows] = (
                q_in[block, :, columns].astype(jnp.float32) + bias[0:1, columns]
            ).astype(jnp.bfloat16)
            g_stack[rows] = g_in[block, :, columns]
        grad_q_turned[...] = jnp.zeros_like(grad_q_turned)
        lines = rows_in[block]
        lse_line = jnp.concatenate([lines[h : h + 1] for h in range(GROUP)], axis=1)
        delta_line = jnp.concatenate([lines[GROUP + h : GROUP + h + 1] for h in range(GROUP)], axis=1)
        q_pos = positions(block, q_local)

        def over_keys(owner, _):
            queries, gradients = q_stack[...], g_stack[...]
            scores = lax.dot_general(
                k_all[owner], queries, NT, preferred_element_type=jnp.float32
            )
            causal = positions(owner, k_local) <= q_pos
            prob = jnp.where(causal, jnp.exp(scores * scale - lse_line), 0.0)
            grad_prob = lax.dot_general(
                v_all[owner], gradients, NT, preferred_element_type=jnp.float32
            )
            score_low = (prob * (grad_prob - delta_line)).astype(jnp.bfloat16)
            prob_low = prob.astype(jnp.bfloat16)
            grad_v[owner] += lax.dot_general(
                prob_low, gradients, NN, preferred_element_type=jnp.float32
            )
            grad_k[owner] += lax.dot_general(
                score_low, queries, NN, preferred_element_type=jnp.float32
            )
            grad_q_turned[...] += lax.dot_general(
                k_turned[owner], score_low, NN, preferred_element_type=jnp.float32
            )
            return 0

        lax.fori_loop(0, n_ctx, over_keys, 0)
        for head in range(GROUP):
            grad_q = grad_q_turned[:, head * tokens : (head + 1) * tokens].T * scale
            head_sums[head] += jnp.sum(grad_q, axis=0, keepdims=True)
            q_out[block, :, head * HEAD_SIZE : (head + 1) * HEAD_SIZE] = grad_q.astype(jnp.bfloat16)

        @pl.when(has_before)
        def _():
            out_copies(block, me)[0].start()

    key_sum = jnp.zeros((1, HEAD_SIZE), jnp.float32)
    value_sum = jnp.zeros((1, HEAD_SIZE), jnp.float32)
    for ctx in range(n_ctx):
        key_part = grad_k[ctx] * scale
        k_out[ctx] = key_part.astype(jnp.bfloat16)
        v_out[ctx] = grad_v[ctx].astype(jnp.bfloat16)
        key_sum += jnp.sum(key_part, axis=0, keepdims=True)
        value_sum += jnp.sum(grad_v[ctx], axis=0, keepdims=True)
    blank = jnp.zeros((8 - GROUP - 2, HEAD_SIZE), jnp.float32)
    sums[my_place] = jnp.concatenate(head_sums + [key_sum, value_sum, blank], axis=0)
    for step in range(1, everyone):
        place = (my_place + step) % everyone
        sum_copy(place, my_place).start()

    @pl.when(has_before)
    def _():
        for step in reversed(range(n_ctx)):
            for copy in out_copies(partner(me, step, n_ctx), me)[1:]:
                copy.start()

    @pl.when(section == n_section - 1)
    def _():
        o_own[...] = jnp.zeros_like(o_own)
        blanks = [
            pltpu.make_async_copy(o_own, rq_ref.at[0, 0], local_sem.at[0]),
            pltpu.make_async_copy(
                o_own.at[:, : KEY_VALUE_HEADS * HEAD_SIZE], rk_ref.at[0, 0], local_sem.at[1]
            ),
            pltpu.make_async_copy(
                o_own.at[:, : KEY_VALUE_HEADS * HEAD_SIZE], rv_ref.at[0, 0], local_sem.at[2]
            ),
        ]
        for copy in blanks:
            copy.start()
        for copy in blanks:
            copy.wait()

    for step in range(1, everyone):
        place = (my_place + step) % everyone
        sum_copy(place, place).wait_recv()
    for ctx in range(n_ctx):
        total = sums[ctx]
        for other in range(1, n_dp):
            total += sums[other * n_ctx + ctx]
        for head in range(GROUP):
            start = ctx * GROUP_WIDTH + head * HEAD_SIZE
            sum_q_ref[:, start : start + HEAD_SIZE] = total[head : head + 1]
        narrow = slice(ctx * HEAD_SIZE, (ctx + 1) * HEAD_SIZE)
        sum_k_ref[:, narrow] = total[GROUP : GROUP + 1]
        sum_v_ref[:, narrow] = total[GROUP + 1 : GROUP + 2]

    for step in range(1, n_ctx):
        for item in range(5):
            in_copy(item, partner(me, step, n_ctx), me).wait_send()
    for step in range(1, everyone):
        sum_copy((my_place + step) % everyone, my_place).wait_send()

    @pl.when(has_before)
    def _():
        for ctx in range(n_ctx):
            for copy in out_copies(ctx, me):
                copy.wait_send()

    @pl.when(has_after)
    def _():
        for ctx in range(n_ctx):
            for copy in out_copies(ctx, ctx):
                copy.wait_recv()


def solution(mesh):
    n_section, n_ctx, n_dp = mesh.shape["section"], mesh.shape["ctx"], mesh.shape["dp"]
    assert n_ctx == KEY_VALUE_HEADS

    def body(q_in, key_in, value_in, out_saved, out_grad, lse, bias_q, key_bias, value_bias):
        tokens = q_in.shape[2]
        width_q, width_k = QUERY_HEADS * HEAD_SIZE, KEY_VALUE_HEADS * HEAD_SIZE
        everyone = n_ctx * n_dp
        anywhere = pl.BlockSpec(memory_space=pl.ANY)
        vmem = pl.BlockSpec(memory_space=pltpu.VMEM)
        low, full = jnp.bfloat16, jnp.float32
        return pl.pallas_call(
            functools.partial(kernel, n_section, n_ctx, n_dp),
            out_shape=(
                jax.ShapeDtypeStruct((1, 1, tokens, width_q), low),
                jax.ShapeDtypeStruct((1, 1, tokens, width_k), low),
                jax.ShapeDtypeStruct((1, 1, tokens, width_k), low),
                jax.ShapeDtypeStruct((1, width_q), full),
                jax.ShapeDtypeStruct((1, width_k), full),
                jax.ShapeDtypeStruct((1, width_k), full),
            ),
            in_specs=[anywhere] * 5 + [vmem] * 4,
            out_specs=(anywhere, anywhere, anywhere, vmem, vmem, vmem),
            scratch_shapes=[
                pltpu.VMEM((n_ctx, tokens, GROUP_WIDTH), low),
                pltpu.VMEM((n_ctx, tokens, GROUP_WIDTH), low),
                pltpu.VMEM((n_ctx, tokens, HEAD_SIZE), low),
                pltpu.VMEM((n_ctx, tokens, HEAD_SIZE), low),
                pltpu.VMEM((n_ctx, 2 * GROUP, tokens), full),
                pltpu.VMEM((n_ctx, 2 * GROUP, tokens), full),
                pltpu.VMEM((tokens, width_q), low),
                pltpu.VMEM((tokens, width_q), low),
                pltpu.VMEM((8, GROUP_WIDTH), full),
                pltpu.VMEM((n_ctx, tokens, HEAD_SIZE), low),
                pltpu.VMEM((n_ctx, tokens, HEAD_SIZE), low),
                pltpu.VMEM((n_ctx, HEAD_SIZE, tokens), low),
                pltpu.VMEM((n_ctx, tokens, HEAD_SIZE), full),
                pltpu.VMEM((n_ctx, tokens, HEAD_SIZE), full),
                pltpu.VMEM((HEAD_SIZE, GROUP * tokens), full),
                pltpu.VMEM((GROUP * tokens, HEAD_SIZE), low),
                pltpu.VMEM((GROUP * tokens, HEAD_SIZE), low),
                pltpu.VMEM((n_ctx, tokens, GROUP_WIDTH), low),
                pltpu.VMEM((n_ctx, tokens, HEAD_SIZE), low),
                pltpu.VMEM((n_ctx, tokens, HEAD_SIZE), low),
                pltpu.VMEM((everyone, 8, HEAD_SIZE), full),
                pltpu.SemaphoreType.DMA((n_ctx, 5)),
                pltpu.SemaphoreType.DMA((n_ctx, 5)),
                pltpu.SemaphoreType.DMA((n_ctx, 3)),
                pltpu.SemaphoreType.DMA((n_ctx, 3)),
                pltpu.SemaphoreType.DMA((everyone,)),
                pltpu.SemaphoreType.DMA((everyone,)),
                pltpu.SemaphoreType.DMA((6,)),
            ],
            compiler_params=pltpu.CompilerParams(
                collective_id=0, has_side_effects=True, vmem_limit_bytes=40 * 1024 * 1024
            ),
        )(q_in, key_in, value_in, out_saved, out_grad, lse, bias_q, key_bias, value_bias)

    rows = P("dp", "section", "ctx", None)
    line = P("section", None)
    return jax.shard_map(
        body,
        mesh=mesh,
        in_specs=(rows,) * 5 + (P("dp", "section", None, "ctx"),) + (line,) * 3,
        out_specs=(rows,) * 3 + (line,) * 3,
        check_vma=False,
    )
```

```python
import functools
import math

import jax
import jax.numpy as jnp
from jax import lax
from jax.experimental import pallas as pl
from jax.experimental.pallas import tpu as pltpu
from jax.sharding import PartitionSpec as P

QUERY_HEADS = 16
KEY_VALUE_HEADS = 4
HEAD_SIZE = 128
GROUP = QUERY_HEADS // KEY_VALUE_HEADS
GROUP_WIDTH = GROUP * HEAD_SIZE
MESH = pl.DeviceIdType.MESH
NT = (((1,), (1,)), ((), ()))
NN = (((1,), (0,)), ((), ()))


def partner(me, step, size):
    if size == 4:
        high, low = me // 2, me % 2
        high = 1 - high if step // 2 else high
        low = 1 - low if step % 2 else low
        return 2 * high + low
    return (me + step) % size


def kernel(
    n_section,
    n_ctx,
    n_dp,
    q_ref,
    k_ref,
    v_ref,
    o_ref,
    g_ref,
    lse_far,
    bq_far,
    bk_far,
    bv_far,
    rq_ref,
    rk_ref,
    rv_ref,
    sum_q_ref,
    sum_k_ref,
    sum_v_ref,
    q_in,
    g_in,
    k_in,
    v_in,
    rows_in,
    rows_out,
    o_own,
    g_own,
    bias,
    k_all,
    v_all,
    k_turned,
    grad_k,
    grad_v,
    grad_q_turned,
    q_stack,
    g_stack,
    q_out,
    k_out,
    v_out,
    sums,
    in_send,
    in_recv,
    out_send,
    out_recv,
    sum_send,
    sum_recv,
    local_sem,
    lse_ref,
    bq_ref,
    bk_ref,
    bv_ref,
):
    tokens = q_in.shape[1]
    half = tokens // 2
    scale = 1.0 / math.sqrt(HEAD_SIZE)
    section = lax.axis_index("section")
    me = lax.axis_index("ctx")
    replica = lax.axis_index("dp")
    everyone = n_ctx * n_dp
    my_place = replica * n_ctx + me
    has_before = section > 0
    has_after = section < n_section - 1

    def ctx_device(ctx):
        return {"section": section, "ctx": ctx, "dp": replica}

    def before_device(ctx):
        return {"section": section - 1, "ctx": ctx, "dp": replica}

    def after_device(ctx):
        return {"section": section + 1, "ctx": ctx, "dp": replica}

    def place_device(place):
        return {"section": section, "ctx": place % n_ctx, "dp": place // n_ctx}

    def group_columns(ctx, width):
        return pl.ds(pl.multiple_of(ctx * width, width), width)

    def sources(ctx):
        wide, narrow = group_columns(ctx, GROUP_WIDTH), group_columns(ctx, HEAD_SIZE)
        return (
            (k_ref.at[0, 0, :, narrow], k_in),
            (v_ref.at[0, 0, :, narrow], v_in),
            (q_ref.at[0, 0, :, wide], q_in),
            (g_ref.at[0, 0, :, wide], g_in),
            (rows_out.at[ctx], rows_in),
        )

    def in_copy(item, to, slot):
        source, target = sources(to)[item]
        return pltpu.make_async_remote_copy(
            src_ref=source,
            dst_ref=target.at[slot],
            send_sem=in_send.at[to, item],
            recv_sem=in_recv.at[slot, item],
            device_id=ctx_device(to),
            device_id_type=MESH,
        )

    def own_copy(item):
        source, target = sources(me)[item]
        return pltpu.make_async_copy(source, target.at[me], local_sem.at[item])

    def out_copies(ctx, slot):
        wide, narrow = group_columns(slot, GROUP_WIDTH), group_columns(slot, HEAD_SIZE)
        return [
            pltpu.make_async_remote_copy(
                src_ref=source.at[ctx],
                dst_ref=target,
                send_sem=out_send.at[ctx, item],
                recv_sem=out_recv.at[slot, item],
                device_id=before_device(ctx),
                device_id_type=MESH,
            )
            for item, (source, target) in enumerate(
                (
                    (q_out, rq_ref.at[0, 0, :, wide]),
                    (k_out, rk_ref.at[0, 0, :, narrow]),
                    (v_out, rv_ref.at[0, 0, :, narrow]),
                )
            )
        ]

    def sum_copy(place, slot):
        return pltpu.make_async_remote_copy(
            src_ref=sums.at[my_place],
            dst_ref=sums.at[slot],
            send_sem=sum_send.at[place],
            recv_sem=sum_recv.at[slot],
            device_id=place_device(place),
            device_id_type=MESH,
        )

    o_copy = pltpu.make_async_copy(o_ref.at[0, 0], o_own, local_sem.at[4])
    g_copy = pltpu.make_async_copy(g_ref.at[0, 0], g_own, local_sem.at[5])

    small_copies = [
        pltpu.make_async_copy(source, target, local_sem.at[6 + item])
        for item, (source, target) in enumerate(
            ((lse_far, lse_ref), (bq_far, bq_ref), (bk_far, bk_ref), (bv_far, bv_ref))
        )
    ]

    barrier = pltpu.get_barrier_semaphore()
    for step in range(1, everyone):
        pl.semaphore_signal(
            barrier,
            inc=1,
            device_id=place_device((my_place + step) % everyone),
            device_id_type=MESH,
        )

    @pl.when(has_before)
    def _():
        for ctx in range(n_ctx):
            pl.semaphore_signal(barrier, inc=1, device_id=before_device(ctx), device_id_type=MESH)

    @pl.when(has_after)
    def _():
        for ctx in range(n_ctx):
            pl.semaphore_signal(barrier, inc=1, device_id=after_device(ctx), device_id_type=MESH)

    o_copy.start()
    g_copy.start()
    for copy in small_copies:
        copy.start()
    for item in range(4):
        own_copy(item).start()
    bias[:, :GROUP_WIDTH] = jnp.zeros((8, GROUP_WIDTH), jnp.float32)

    neighbours = jnp.where(has_before, n_ctx, 0) + jnp.where(has_after, n_ctx, 0)
    pl.semaphore_wait(barrier, everyone - 1 + neighbours)

    for items in ((0, 1), (2, 3)):
        for step in reversed(range(1, n_ctx)):
            for item in items:
                in_copy(item, partner(me, step, n_ctx), me).start()

    o_copy.wait()
    g_copy.wait()
    for copy in small_copies:
        copy.wait()
    for group in range(KEY_VALUE_HEADS):
        lines = [lse_ref[0, 0, pl.ds(group * GROUP, GROUP), :]]
        for head in range(group * GROUP, (group + 1) * GROUP):
            columns = slice(head * HEAD_SIZE, (head + 1) * HEAD_SIZE)
            product = g_own[:, columns].astype(jnp.float32) * o_own[:, columns].astype(jnp.float32)
            lines.append(jnp.sum(product.T, axis=0, keepdims=True))
        rows_out[group] = jnp.concatenate(lines, axis=0)
    for step in reversed(range(1, n_ctx)):
        in_copy(4, partner(me, step, n_ctx), me).start()
    rows_in[me] = rows_out[me]

    for ctx in range(n_ctx):
        wide = slice(ctx * GROUP_WIDTH, (ctx + 1) * GROUP_WIDTH)
        narrow = slice(ctx * HEAD_SIZE, (ctx + 1) * HEAD_SIZE)

        @pl.when(me == ctx)
        def _():
            bias[0:1, :] = bq_ref[:, wide].astype(jnp.float32)
            bias[1:2, :HEAD_SIZE] = bk_ref[:, narrow].astype(jnp.float32)
            bias[2:3, :HEAD_SIZE] = bv_ref[:, narrow].astype(jnp.float32)

    for item in range(4):
        own_copy(item).wait()
    for step in range(1, n_ctx):
        for item in (0, 1):
            in_copy(item, partner(me, step, n_ctx), partner(me, step, n_ctx)).wait_recv()
    for ctx in range(n_ctx):
        k_low = (k_in[ctx].astype(jnp.float32) + bias[1:2, :HEAD_SIZE]).astype(jnp.bfloat16)
        k_all[ctx] = k_low
        k_turned[ctx] = k_low.astype(jnp.float32).T.astype(jnp.bfloat16)
        v_all[ctx] = (v_in[ctx].astype(jnp.float32) + bias[2:3, :HEAD_SIZE]).astype(jnp.bfloat16)
    grad_k[...] = jnp.zeros_like(grad_k)
    grad_v[...] = jnp.zeros_like(grad_v)

    def positions(block, local):
        late = (2 * n_ctx - 1 - block) * half + local - half
        return jnp.where(local < half, block * half + local, late)

    q_local = jnp.concatenate(
        [lax.broadcasted_iota(jnp.int32, (1, tokens), 1)] * GROUP, axis=1
    )
    k_local = lax.broadcasted_iota(jnp.int32, (tokens, 1), 0)
    head_sums = [jnp.zeros((1, HEAD_SIZE), jnp.float32) for _ in range(GROUP)]

    for step in range(n_ctx):
        block = partner(me, step, n_ctx)
        if step:
            for item in (2, 3, 4):
                in_copy(item, block, block).wait_recv()
        for head in range(GROUP):
            columns = slice(head * HEAD_SIZE, (head + 1) * HEAD_SIZE)
            rows = slice(head * tokens, (head + 1) * tokens)
            q_stack[rows] = (
                q_in[block, :, columns].astype(jnp.float32) + bias[0:1, columns]
            ).astype(jnp.bfloat16)
            g_stack[rows] = g_in[block, :, columns]
        grad_q_turned[...] = jnp.zeros_like(grad_q_turned)
        lines = rows_in[block]
        lse_line = jnp.concatenate([lines[h : h + 1] for h in range(GROUP)], axis=1)
        delta_line = jnp.concatenate([lines[GROUP + h : GROUP + h + 1] for h in range(GROUP)], axis=1)
        q_pos = positions(block, q_local)

        def over_keys(owner, _):
            queries, gradients = q_stack[...], g_stack[...]
            scores = lax.dot_general(
                k_all[owner], queries, NT, preferred_element_type=jnp.float32
            )
            causal = positions(owner, k_local) <= q_pos
            prob = jnp.where(causal, jnp.exp(scores * scale - lse_line), 0.0)
            grad_prob = lax.dot_general(
                v_all[owner], gradients, NT, preferred_element_type=jnp.float32
            )
            score_low = (prob * (grad_prob - delta_line)).astype(jnp.bfloat16)
            prob_low = prob.astype(jnp.bfloat16)
            grad_v[owner] += lax.dot_general(
                prob_low, gradients, NN, preferred_element_type=jnp.float32
            )
            grad_k[owner] += lax.dot_general(
                score_low, queries, NN, preferred_element_type=jnp.float32
            )
            grad_q_turned[...] += lax.dot_general(
                k_turned[owner], score_low, NN, preferred_element_type=jnp.float32
            )
            return 0

        lax.fori_loop(0, n_ctx, over_keys, 0)
        for head in range(GROUP):
            grad_q = grad_q_turned[:, head * tokens : (head + 1) * tokens].T * scale
            head_sums[head] += jnp.sum(grad_q, axis=0, keepdims=True)
            q_out[block, :, head * HEAD_SIZE : (head + 1) * HEAD_SIZE] = grad_q.astype(jnp.bfloat16)

        @pl.when(has_before)
        def _():
            out_copies(block, me)[0].start()

    key_sum = jnp.zeros((1, HEAD_SIZE), jnp.float32)
    value_sum = jnp.zeros((1, HEAD_SIZE), jnp.float32)
    for ctx in range(n_ctx):
        key_part = grad_k[ctx] * scale
        k_out[ctx] = key_part.astype(jnp.bfloat16)
        v_out[ctx] = grad_v[ctx].astype(jnp.bfloat16)
        key_sum += jnp.sum(key_part, axis=0, keepdims=True)
        value_sum += jnp.sum(grad_v[ctx], axis=0, keepdims=True)
    blank = jnp.zeros((8 - GROUP - 2, HEAD_SIZE), jnp.float32)
    sums[my_place] = jnp.concatenate(head_sums + [key_sum, value_sum, blank], axis=0)
    for step in range(1, everyone):
        place = (my_place + step) % everyone
        sum_copy(place, my_place).start()

    @pl.when(has_before)
    def _():
        for step in reversed(range(n_ctx)):
            for copy in out_copies(partner(me, step, n_ctx), me)[1:]:
                copy.start()

    @pl.when(section == n_section - 1)
    def _():
        o_own[...] = jnp.zeros_like(o_own)
        blanks = [
            pltpu.make_async_copy(o_own, rq_ref.at[0, 0], local_sem.at[0]),
            pltpu.make_async_copy(
                o_own.at[:, : KEY_VALUE_HEADS * HEAD_SIZE], rk_ref.at[0, 0], local_sem.at[1]
            ),
            pltpu.make_async_copy(
                o_own.at[:, : KEY_VALUE_HEADS * HEAD_SIZE], rv_ref.at[0, 0], local_sem.at[2]
            ),
        ]
        for copy in blanks:
            copy.start()
        for copy in blanks:
            copy.wait()

    for step in range(1, everyone):
        place = (my_place + step) % everyone
        sum_copy(place, place).wait_recv()
    for ctx in range(n_ctx):
        total = sums[ctx]
        for other in range(1, n_dp):
            total += sums[other * n_ctx + ctx]
        for head in range(GROUP):
            start = ctx * GROUP_WIDTH + head * HEAD_SIZE
            sum_q_ref[:, start : start + HEAD_SIZE] = total[head : head + 1]
        narrow = slice(ctx * HEAD_SIZE, (ctx + 1) * HEAD_SIZE)
        sum_k_ref[:, narrow] = total[GROUP : GROUP + 1]
        sum_v_ref[:, narrow] = total[GROUP + 1 : GROUP + 2]

    for step in range(1, n_ctx):
        for item in range(5):
            in_copy(item, partner(me, step, n_ctx), me).wait_send()
    for step in range(1, everyone):
        sum_copy((my_place + step) % everyone, my_place).wait_send()

    @pl.when(has_before)
    def _():
        for ctx in range(n_ctx):
            for copy in out_copies(ctx, me):
                copy.wait_send()

    @pl.when(has_after)
    def _():
        for ctx in range(n_ctx):
            for copy in out_copies(ctx, ctx):
                copy.wait_recv()


def placing(*refs):
    sources, targets, sems = refs[:6], refs[6:12], refs[12]
    copies = [
        pltpu.make_async_copy(source, target, sems.at[item])
        for item, (source, target) in enumerate(zip(sources, targets))
    ]
    for copy in copies:
        copy.start()
    for copy in copies:
        copy.wait()


def solution(mesh):
    n_section, n_ctx, n_dp = mesh.shape["section"], mesh.shape["ctx"], mesh.shape["dp"]
    assert n_ctx == KEY_VALUE_HEADS

    def body(q_in, key_in, value_in, out_saved, out_grad, lse, bias_q, key_bias, value_bias):
        tokens = q_in.shape[2]
        width_q, width_k = QUERY_HEADS * HEAD_SIZE, KEY_VALUE_HEADS * HEAD_SIZE
        everyone = n_ctx * n_dp
        anywhere = pl.BlockSpec(memory_space=pl.ANY)
        vmem = pl.BlockSpec(memory_space=pltpu.VMEM)
        hbm = pl.BlockSpec(memory_space=pltpu.HBM)
        low, full = jnp.bfloat16, jnp.float32
        results = pl.pallas_call(
            functools.partial(kernel, n_section, n_ctx, n_dp),
            out_shape=(
                jax.ShapeDtypeStruct((1, 1, tokens, width_q), low),
                jax.ShapeDtypeStruct((1, 1, tokens, width_k), low),
                jax.ShapeDtypeStruct((1, 1, tokens, width_k), low),
                jax.ShapeDtypeStruct((1, width_q), full),
                jax.ShapeDtypeStruct((1, width_k), full),
                jax.ShapeDtypeStruct((1, width_k), full),
            ),
            in_specs=[hbm] * 9,
            out_specs=(anywhere, anywhere, anywhere, vmem, vmem, vmem),
            scratch_shapes=[
                pltpu.VMEM((n_ctx, tokens, GROUP_WIDTH), low),
                pltpu.VMEM((n_ctx, tokens, GROUP_WIDTH), low),
                pltpu.VMEM((n_ctx, tokens, HEAD_SIZE), low),
                pltpu.VMEM((n_ctx, tokens, HEAD_SIZE), low),
                pltpu.VMEM((n_ctx, 2 * GROUP, tokens), full),
                pltpu.VMEM((n_ctx, 2 * GROUP, tokens), full),
                pltpu.VMEM((tokens, width_q), low),
                pltpu.VMEM((tokens, width_q), low),
                pltpu.VMEM((8, GROUP_WIDTH), full),
                pltpu.VMEM((n_ctx, tokens, HEAD_SIZE), low),
                pltpu.VMEM((n_ctx, tokens, HEAD_SIZE), low),
                pltpu.VMEM((n_ctx, HEAD_SIZE, tokens), low),
                pltpu.VMEM((n_ctx, tokens, HEAD_SIZE), full),
                pltpu.VMEM((n_ctx, tokens, HEAD_SIZE), full),
                pltpu.VMEM((HEAD_SIZE, GROUP * tokens), full),
                pltpu.VMEM((GROUP * tokens, HEAD_SIZE), low),
                pltpu.VMEM((GROUP * tokens, HEAD_SIZE), low),
                pltpu.VMEM((n_ctx, tokens, GROUP_WIDTH), low),
                pltpu.VMEM((n_ctx, tokens, HEAD_SIZE), low),
                pltpu.VMEM((n_ctx, tokens, HEAD_SIZE), low),
                pltpu.VMEM((everyone, 8, HEAD_SIZE), full),
                pltpu.SemaphoreType.DMA((n_ctx, 5)),
                pltpu.SemaphoreType.DMA((n_ctx, 5)),
                pltpu.SemaphoreType.DMA((n_ctx, 3)),
                pltpu.SemaphoreType.DMA((n_ctx, 3)),
                pltpu.SemaphoreType.DMA((everyone,)),
                pltpu.SemaphoreType.DMA((everyone,)),
                pltpu.SemaphoreType.DMA((10,)),
                pltpu.VMEM(lse.shape, full),
                pltpu.VMEM(bias_q.shape, low),
                pltpu.VMEM(key_bias.shape, low),
                pltpu.VMEM(value_bias.shape, low),
            ],
            compiler_params=pltpu.CompilerParams(
                collective_id=0, has_side_effects=True, vmem_limit_bytes=64 * 1024 * 1024
            ),
        )(q_in, key_in, value_in, out_saved, out_grad, lse, bias_q, key_bias, value_bias)
        return pl.pallas_call(
            placing,
            out_shape=tuple(jax.ShapeDtypeStruct(r.shape, r.dtype) for r in results),
            in_specs=[anywhere] * 6,
            out_specs=(hbm,) * 6,
            scratch_shapes=[pltpu.SemaphoreType.DMA((6,))],
            compiler_params=pltpu.CompilerParams(vmem_limit_bytes=64 * 1024 * 1024),
        )(*results)

    rows = P("dp", "section", "ctx", None)
    line = P("section", None)
    return jax.shard_map(
        body,
        mesh=mesh,
        in_specs=(rows,) * 5 + (P("dp", "section", None, "ctx"),) + (line,) * 3,
        out_specs=(rows,) * 3 + (line,) * 3,
        check_vma=False,
    )
```

```python
import functools
import math

import jax
import jax.numpy as jnp
from jax import lax
from jax.experimental import pallas as pl
from jax.experimental.pallas import tpu as pltpu
from jax.sharding import PartitionSpec as P

QUERY_HEADS = 16
KEY_VALUE_HEADS = 4
HEAD_SIZE = 128
GROUP = QUERY_HEADS // KEY_VALUE_HEADS
GROUP_WIDTH = GROUP * HEAD_SIZE
MESH = pl.DeviceIdType.MESH
NT = (((1,), (1,)), ((), ()))
NN = (((1,), (0,)), ((), ()))


def partner(me, step, size):
    if size == 4:
        high, low = me // 2, me % 2
        high = 1 - high if step // 2 else high
        low = 1 - low if step % 2 else low
        return 2 * high + low
    return (me + step) % size


def kernel(
    n_section,
    n_ctx,
    n_dp,
    q_ref,
    k_ref,
    v_ref,
    o_ref,
    g_ref,
    lse_far,
    bq_far,
    bk_far,
    bv_far,
    rq_ref,
    rk_ref,
    rv_ref,
    sum_q_ref,
    sum_k_ref,
    sum_v_ref,
    q_in,
    g_in,
    k_in,
    v_in,
    rows_in,
    rows_out,
    o_own,
    g_own,
    bias,
    k_all,
    v_all,
    k_turned,
    grad_k,
    grad_v,
    grad_q_turned,
    q_stack,
    g_stack,
    q_out,
    k_out,
    v_out,
    sums,
    in_send,
    in_recv,
    out_send,
    out_recv,
    sum_send,
    sum_recv,
    local_sem,
    lse_ref,
    bq_ref,
    bk_ref,
    bv_ref,
):
    tokens = q_in.shape[1]
    half = tokens // 2
    scale = 1.0 / math.sqrt(HEAD_SIZE)
    section = lax.axis_index("section")
    me = lax.axis_index("ctx")
    replica = lax.axis_index("dp")
    everyone = n_ctx * n_dp
    my_place = replica * n_ctx + me
    has_before = section > 0
    has_after = section < n_section - 1

    def ctx_device(ctx):
        return {"section": section, "ctx": ctx, "dp": replica}

    def before_device(ctx):
        return {"section": section - 1, "ctx": ctx, "dp": replica}

    def after_device(ctx):
        return {"section": section + 1, "ctx": ctx, "dp": replica}

    def place_device(place):
        return {"section": section, "ctx": place % n_ctx, "dp": place // n_ctx}

    def group_columns(ctx, width):
        return pl.ds(pl.multiple_of(ctx * width, width), width)

    def sources(ctx):
        wide, narrow = group_columns(ctx, GROUP_WIDTH), group_columns(ctx, HEAD_SIZE)
        return (
            (k_ref.at[0, 0, :, narrow], k_in),
            (v_ref.at[0, 0, :, narrow], v_in),
            (q_ref.at[0, 0, :, wide], q_in),
            (g_ref.at[0, 0, :, wide], g_in),
            (rows_out.at[ctx], rows_in),
        )

    def in_copy(item, to, slot):
        source, target = sources(to)[item]
        return pltpu.make_async_remote_copy(
            src_ref=source,
            dst_ref=target.at[slot],
            send_sem=in_send.at[to, item],
            recv_sem=in_recv.at[slot, item],
            device_id=ctx_device(to),
            device_id_type=MESH,
        )

    def own_copy(item):
        source, target = sources(me)[item]
        return pltpu.make_async_copy(source, target.at[me], local_sem.at[item])

    def out_copies(ctx, slot):
        wide, narrow = group_columns(slot, GROUP_WIDTH), group_columns(slot, HEAD_SIZE)
        return [
            pltpu.make_async_remote_copy(
                src_ref=source.at[ctx],
                dst_ref=target,
                send_sem=out_send.at[ctx, item],
                recv_sem=out_recv.at[slot, item],
                device_id=before_device(ctx),
                device_id_type=MESH,
            )
            for item, (source, target) in enumerate(
                (
                    (q_out, rq_ref.at[0, 0, :, wide]),
                    (k_out, rk_ref.at[0, 0, :, narrow]),
                    (v_out, rv_ref.at[0, 0, :, narrow]),
                )
            )
        ]

    def sum_copy(place, slot):
        return pltpu.make_async_remote_copy(
            src_ref=sums.at[my_place],
            dst_ref=sums.at[slot],
            send_sem=sum_send.at[place],
            recv_sem=sum_recv.at[slot],
            device_id=place_device(place),
            device_id_type=MESH,
        )

    o_copy = pltpu.make_async_copy(o_ref.at[0, 0], o_own, local_sem.at[4])
    g_copy = pltpu.make_async_copy(g_ref.at[0, 0], g_own, local_sem.at[5])

    small_copies = [
        pltpu.make_async_copy(source, target, local_sem.at[6 + item])
        for item, (source, target) in enumerate(
            ((lse_far, lse_ref), (bq_far, bq_ref), (bk_far, bk_ref), (bv_far, bv_ref))
        )
    ]

    barrier = pltpu.get_barrier_semaphore()
    for step in range(1, everyone):
        pl.semaphore_signal(
            barrier,
            inc=1,
            device_id=place_device((my_place + step) % everyone),
            device_id_type=MESH,
        )

    @pl.when(has_before)
    def _():
        for ctx in range(n_ctx):
            pl.semaphore_signal(barrier, inc=1, device_id=before_device(ctx), device_id_type=MESH)

    @pl.when(has_after)
    def _():
        for ctx in range(n_ctx):
            pl.semaphore_signal(barrier, inc=1, device_id=after_device(ctx), device_id_type=MESH)

    o_copy.start()
    g_copy.start()
    for copy in small_copies:
        copy.start()
    for item in range(4):
        own_copy(item).start()
    bias[:, :GROUP_WIDTH] = jnp.zeros((8, GROUP_WIDTH), jnp.float32)

    neighbours = jnp.where(has_before, n_ctx, 0) + jnp.where(has_after, n_ctx, 0)
    pl.semaphore_wait(barrier, everyone - 1 + neighbours)

    for items in ((0, 1), (2, 3)):
        for step in reversed(range(1, n_ctx)):
            for item in items:
                in_copy(item, partner(me, step, n_ctx), me).start()

    o_copy.wait()
    g_copy.wait()
    for copy in small_copies:
        copy.wait()
    for group in range(KEY_VALUE_HEADS):
        lines = [lse_ref[0, 0, pl.ds(group * GROUP, GROUP), :]]
        for head in range(group * GROUP, (group + 1) * GROUP):
            columns = slice(head * HEAD_SIZE, (head + 1) * HEAD_SIZE)
            product = g_own[:, columns].astype(jnp.float32) * o_own[:, columns].astype(jnp.float32)
            lines.append(jnp.sum(product.T, axis=0, keepdims=True))
        rows_out[group] = jnp.concatenate(lines, axis=0)
    for step in reversed(range(1, n_ctx)):
        in_copy(4, partner(me, step, n_ctx), me).start()
    rows_in[me] = rows_out[me]

    for ctx in range(n_ctx):
        wide = slice(ctx * GROUP_WIDTH, (ctx + 1) * GROUP_WIDTH)
        narrow = slice(ctx * HEAD_SIZE, (ctx + 1) * HEAD_SIZE)

        @pl.when(me == ctx)
        def _():
            bias[0:1, :] = bq_ref[:, wide].astype(jnp.float32)
            bias[1:2, :HEAD_SIZE] = bk_ref[:, narrow].astype(jnp.float32)
            bias[2:3, :HEAD_SIZE] = bv_ref[:, narrow].astype(jnp.float32)

    for item in range(4):
        own_copy(item).wait()
    for step in range(1, n_ctx):
        for item in (0, 1):
            in_copy(item, partner(me, step, n_ctx), partner(me, step, n_ctx)).wait_recv()
    for ctx in range(n_ctx):
        k_low = (k_in[ctx].astype(jnp.float32) + bias[1:2, :HEAD_SIZE]).astype(jnp.bfloat16)
        k_all[ctx] = k_low
        k_turned[ctx] = k_low.astype(jnp.float32).T.astype(jnp.bfloat16)
        v_all[ctx] = (v_in[ctx].astype(jnp.float32) + bias[2:3, :HEAD_SIZE]).astype(jnp.bfloat16)
    grad_k[...] = jnp.zeros_like(grad_k)
    grad_v[...] = jnp.zeros_like(grad_v)

    def positions(block, local):
        late = (2 * n_ctx - 1 - block) * half + local - half
        return jnp.where(local < half, block * half + local, late)

    q_local = jnp.concatenate(
        [lax.broadcasted_iota(jnp.int32, (1, tokens), 1)] * GROUP, axis=1
    )
    k_local = lax.broadcasted_iota(jnp.int32, (tokens, 1), 0)
    head_sums = [jnp.zeros((1, HEAD_SIZE), jnp.float32) for _ in range(GROUP)]

    for step in [0] + list(reversed(range(1, n_ctx))):
        block = partner(me, step, n_ctx)
        if step:
            for item in (2, 3, 4):
                in_copy(item, block, block).wait_recv()
        for head in range(GROUP):
            columns = slice(head * HEAD_SIZE, (head + 1) * HEAD_SIZE)
            rows = slice(head * tokens, (head + 1) * tokens)
            q_stack[rows] = (
                q_in[block, :, columns].astype(jnp.float32) + bias[0:1, columns]
            ).astype(jnp.bfloat16)
            g_stack[rows] = g_in[block, :, columns]
        grad_q_turned[...] = jnp.zeros_like(grad_q_turned)
        lines = rows_in[block]
        lse_line = jnp.concatenate([lines[h : h + 1] for h in range(GROUP)], axis=1)
        delta_line = jnp.concatenate([lines[GROUP + h : GROUP + h + 1] for h in range(GROUP)], axis=1)
        q_pos = positions(block, q_local)

        def over_keys(owner, _):
            queries, gradients = q_stack[...], g_stack[...]
            scores = lax.dot_general(
                k_all[owner], queries, NT, preferred_element_type=jnp.float32
            )
            causal = positions(owner, k_local) <= q_pos
            prob = jnp.where(causal, jnp.exp(scores * scale - lse_line), 0.0)
            grad_prob = lax.dot_general(
                v_all[owner], gradients, NT, preferred_element_type=jnp.float32
            )
            score_low = (prob * (grad_prob - delta_line)).astype(jnp.bfloat16)
            prob_low = prob.astype(jnp.bfloat16)
            grad_v[owner] += lax.dot_general(
                prob_low, gradients, NN, preferred_element_type=jnp.float32
            )
            grad_k[owner] += lax.dot_general(
                score_low, queries, NN, preferred_element_type=jnp.float32
            )
            grad_q_turned[...] += lax.dot_general(
                k_turned[owner], score_low, NN, preferred_element_type=jnp.float32
            )
            return 0

        lax.fori_loop(0, n_ctx, over_keys, 0)
        for head in range(GROUP):
            grad_q = grad_q_turned[:, head * tokens : (head + 1) * tokens].T * scale
            head_sums[head] += jnp.sum(grad_q, axis=0, keepdims=True)
            q_out[block, :, head * HEAD_SIZE : (head + 1) * HEAD_SIZE] = grad_q.astype(jnp.bfloat16)

        @pl.when(has_before)
        def _():
            out_copies(block, me)[0].start()

    key_sum = jnp.zeros((1, HEAD_SIZE), jnp.float32)
    value_sum = jnp.zeros((1, HEAD_SIZE), jnp.float32)
    for ctx in range(n_ctx):
        key_part = grad_k[ctx] * scale
        k_out[ctx] = key_part.astype(jnp.bfloat16)
        v_out[ctx] = grad_v[ctx].astype(jnp.bfloat16)
        key_sum += jnp.sum(key_part, axis=0, keepdims=True)
        value_sum += jnp.sum(grad_v[ctx], axis=0, keepdims=True)
    blank = jnp.zeros((8 - GROUP - 2, HEAD_SIZE), jnp.float32)
    sums[my_place] = jnp.concatenate(head_sums + [key_sum, value_sum, blank], axis=0)
    for step in range(1, everyone):
        place = (my_place + step) % everyone
        sum_copy(place, my_place).start()

    @pl.when(has_before)
    def _():
        for step in reversed(range(n_ctx)):
            for copy in out_copies(partner(me, step, n_ctx), me)[1:]:
                copy.start()

    @pl.when(section == n_section - 1)
    def _():
        o_own[...] = jnp.zeros_like(o_own)
        blanks = [
            pltpu.make_async_copy(o_own, rq_ref.at[0, 0], local_sem.at[0]),
            pltpu.make_async_copy(
                o_own.at[:, : KEY_VALUE_HEADS * HEAD_SIZE], rk_ref.at[0, 0], local_sem.at[1]
            ),
            pltpu.make_async_copy(
                o_own.at[:, : KEY_VALUE_HEADS * HEAD_SIZE], rv_ref.at[0, 0], local_sem.at[2]
            ),
        ]
        for copy in blanks:
            copy.start()
        for copy in blanks:
            copy.wait()

    for step in range(1, everyone):
        place = (my_place + step) % everyone
        sum_copy(place, place).wait_recv()
    for ctx in range(n_ctx):
        total = sums[ctx]
        for other in range(1, n_dp):
            total += sums[other * n_ctx + ctx]
        for head in range(GROUP):
            start = ctx * GROUP_WIDTH + head * HEAD_SIZE
            sum_q_ref[:, start : start + HEAD_SIZE] = total[head : head + 1]
        narrow = slice(ctx * HEAD_SIZE, (ctx + 1) * HEAD_SIZE)
        sum_k_ref[:, narrow] = total[GROUP : GROUP + 1]
        sum_v_ref[:, narrow] = total[GROUP + 1 : GROUP + 2]

    for step in range(1, n_ctx):
        for item in range(5):
            in_copy(item, partner(me, step, n_ctx), me).wait_send()
    for step in range(1, everyone):
        sum_copy((my_place + step) % everyone, my_place).wait_send()

    @pl.when(has_before)
    def _():
        for ctx in range(n_ctx):
            for copy in out_copies(ctx, me):
                copy.wait_send()

    @pl.when(has_after)
    def _():
        for ctx in range(n_ctx):
            for copy in out_copies(ctx, ctx):
                copy.wait_recv()


def placing(*refs):
    sources, targets, held, sems = refs[:6], refs[6:12], refs[12:18], refs[18]
    fetches = [
        pltpu.make_async_copy(source, slot, sems.at[0, item])
        for item, (source, slot) in enumerate(zip(sources, held))
    ]
    stores = [
        pltpu.make_async_copy(slot, target, sems.at[1, item])
        for item, (slot, target) in enumerate(zip(held, targets))
    ]
    for copy in fetches:
        copy.start()
    for fetch, store in zip(fetches, stores):
        fetch.wait()
        store.start()
    for copy in stores:
        copy.wait()


def solution(mesh):
    n_section, n_ctx, n_dp = mesh.shape["section"], mesh.shape["ctx"], mesh.shape["dp"]
    assert n_ctx == KEY_VALUE_HEADS

    def body(q_in, key_in, value_in, out_saved, out_grad, lse, bias_q, key_bias, value_bias):
        tokens = q_in.shape[2]
        width_q, width_k = QUERY_HEADS * HEAD_SIZE, KEY_VALUE_HEADS * HEAD_SIZE
        everyone = n_ctx * n_dp
        anywhere = pl.BlockSpec(memory_space=pl.ANY)
        vmem = pl.BlockSpec(memory_space=pltpu.VMEM)
        hbm = pl.BlockSpec(memory_space=pltpu.HBM)
        low, full = jnp.bfloat16, jnp.float32
        results = pl.pallas_call(
            functools.partial(kernel, n_section, n_ctx, n_dp),
            out_shape=(
                jax.ShapeDtypeStruct((1, 1, tokens, width_q), low),
                jax.ShapeDtypeStruct((1, 1, tokens, width_k), low),
                jax.ShapeDtypeStruct((1, 1, tokens, width_k), low),
                jax.ShapeDtypeStruct((1, width_q), full),
                jax.ShapeDtypeStruct((1, width_k), full),
                jax.ShapeDtypeStruct((1, width_k), full),
            ),
            in_specs=[hbm] * 9,
            out_specs=(anywhere, anywhere, anywhere, vmem, vmem, vmem),
            scratch_shapes=[
                pltpu.VMEM((n_ctx, tokens, GROUP_WIDTH), low),
                pltpu.VMEM((n_ctx, tokens, GROUP_WIDTH), low),
                pltpu.VMEM((n_ctx, tokens, HEAD_SIZE), low),
                pltpu.VMEM((n_ctx, tokens, HEAD_SIZE), low),
                pltpu.VMEM((n_ctx, 2 * GROUP, tokens), full),
                pltpu.VMEM((n_ctx, 2 * GROUP, tokens), full),
                pltpu.VMEM((tokens, width_q), low),
                pltpu.VMEM((tokens, width_q), low),
                pltpu.VMEM((8, GROUP_WIDTH), full),
                pltpu.VMEM((n_ctx, tokens, HEAD_SIZE), low),
                pltpu.VMEM((n_ctx, tokens, HEAD_SIZE), low),
                pltpu.VMEM((n_ctx, HEAD_SIZE, tokens), low),
                pltpu.VMEM((n_ctx, tokens, HEAD_SIZE), full),
                pltpu.VMEM((n_ctx, tokens, HEAD_SIZE), full),
                pltpu.VMEM((HEAD_SIZE, GROUP * tokens), full),
                pltpu.VMEM((GROUP * tokens, HEAD_SIZE), low),
                pltpu.VMEM((GROUP * tokens, HEAD_SIZE), low),
                pltpu.VMEM((n_ctx, tokens, GROUP_WIDTH), low),
                pltpu.VMEM((n_ctx, tokens, HEAD_SIZE), low),
                pltpu.VMEM((n_ctx, tokens, HEAD_SIZE), low),
                pltpu.VMEM((everyone, 8, HEAD_SIZE), full),
                pltpu.SemaphoreType.DMA((n_ctx, 5)),
                pltpu.SemaphoreType.DMA((n_ctx, 5)),
                pltpu.SemaphoreType.DMA((n_ctx, 3)),
                pltpu.SemaphoreType.DMA((n_ctx, 3)),
                pltpu.SemaphoreType.DMA((everyone,)),
                pltpu.SemaphoreType.DMA((everyone,)),
                pltpu.SemaphoreType.DMA((10,)),
                pltpu.VMEM(lse.shape, full),
                pltpu.VMEM(bias_q.shape, low),
                pltpu.VMEM(key_bias.shape, low),
                pltpu.VMEM(value_bias.shape, low),
            ],
            compiler_params=pltpu.CompilerParams(
                collective_id=0, has_side_effects=True, vmem_limit_bytes=64 * 1024 * 1024
            ),
        )(q_in, key_in, value_in, out_saved, out_grad, lse, bias_q, key_bias, value_bias)
        return pl.pallas_call(
            placing,
            out_shape=tuple(jax.ShapeDtypeStruct(r.shape, r.dtype) for r in results),
            in_specs=[anywhere] * 6,
            out_specs=(hbm,) * 6,
            scratch_shapes=[pltpu.VMEM(r.shape, r.dtype) for r in results]
            + [pltpu.SemaphoreType.DMA((2, 6))],
            compiler_params=pltpu.CompilerParams(vmem_limit_bytes=64 * 1024 * 1024),
        )(*results)

    rows = P("dp", "section", "ctx", None)
    line = P("section", None)
    return jax.shard_map(
        body,
        mesh=mesh,
        in_specs=(rows,) * 5 + (P("dp", "section", None, "ctx"),) + (line,) * 3,
        out_specs=(rows,) * 3 + (line,) * 3,
        check_vma=False,
    )
```

```python
import functools
import math

import jax
import jax.numpy as jnp
from jax import lax
from jax.experimental import pallas as pl
from jax.experimental.pallas import tpu as pltpu
from jax.sharding import PartitionSpec as P

QUERY_HEADS = 16
KEY_VALUE_HEADS = 4
HEAD_SIZE = 128
GROUP = QUERY_HEADS // KEY_VALUE_HEADS
GROUP_WIDTH = GROUP * HEAD_SIZE
PARTS = 2
PART_HEADS = GROUP // PARTS
PART_WIDTH = PART_HEADS * HEAD_SIZE
MESH = pl.DeviceIdType.MESH
NT = (((1,), (1,)), ((), ()))
NN = (((1,), (0,)), ((), ()))


def partner(me, step, size):
    if size == 4:
        high, low = me // 2, me % 2
        high = 1 - high if step // 2 else high
        low = 1 - low if step % 2 else low
        return 2 * high + low
    return (me + step) % size


def kernel(
    n_section,
    n_ctx,
    n_dp,
    q_ref,
    k_ref,
    v_ref,
    o_ref,
    g_ref,
    lse_far,
    bq_far,
    bk_far,
    bv_far,
    rq_ref,
    rk_ref,
    rv_ref,
    sum_q_ref,
    sum_k_ref,
    sum_v_ref,
    q_in,
    g_in,
    k_in,
    v_in,
    rows_in,
    rows_out,
    o_own,
    g_own,
    bias,
    k_all,
    v_all,
    k_turned,
    grad_k,
    grad_v,
    grad_q_turned,
    q_stack,
    g_stack,
    q_out,
    k_out,
    v_out,
    sums,
    in_send,
    in_recv,
    out_send,
    out_recv,
    sum_send,
    sum_recv,
    own_sem,
    local_sem,
    lse_ref,
    bq_ref,
    bk_ref,
    bv_ref,
):
    tokens = k_in.shape[1]
    half = tokens // 2
    in_items, out_items = 3 + 2 * PARTS, PARTS + 2
    scale = 1.0 / math.sqrt(HEAD_SIZE)
    section = lax.axis_index("section")
    me = lax.axis_index("ctx")
    replica = lax.axis_index("dp")
    everyone = n_ctx * n_dp
    my_place = replica * n_ctx + me
    has_before = section > 0
    has_after = section < n_section - 1

    def ctx_device(ctx):
        return {"section": section, "ctx": ctx, "dp": replica}

    def before_device(ctx):
        return {"section": section - 1, "ctx": ctx, "dp": replica}

    def after_device(ctx):
        return {"section": section + 1, "ctx": ctx, "dp": replica}

    def place_device(place):
        return {"section": section, "ctx": place % n_ctx, "dp": place // n_ctx}

    def group_columns(ctx, width):
        return pl.ds(pl.multiple_of(ctx * width, width), width)

    def transfer(item, ctx, slot):
        narrow = group_columns(ctx, HEAD_SIZE)
        if item == 0:
            return k_ref.at[0, 0, :, narrow], k_in.at[slot]
        if item == 1:
            return v_ref.at[0, 0, :, narrow], v_in.at[slot]
        if item == 2:
            return rows_out.at[ctx], rows_in.at[slot]
        part = (item - 3) // 2
        wide = group_columns(ctx * PARTS + part, PART_WIDTH)
        if item % 2:
            return q_ref.at[0, 0, :, wide], q_in.at[slot, part]
        return g_ref.at[0, 0, :, wide], g_in.at[slot, part]

    def in_copy(item, to, slot):
        source, target = transfer(item, to, slot)
        return pltpu.make_async_remote_copy(
            src_ref=source,
            dst_ref=target,
            send_sem=in_send.at[to, item],
            recv_sem=in_recv.at[slot, item],
            device_id=ctx_device(to),
            device_id_type=MESH,
        )

    def own_copy(item):
        source, target = transfer(item, me, me)
        return pltpu.make_async_copy(source, target, own_sem.at[item])

    def out_copy(item, ctx, slot):
        narrow = group_columns(slot, HEAD_SIZE)
        if item < PARTS:
            wide = group_columns(slot * PARTS + item, PART_WIDTH)
            source, target = q_out.at[ctx, item], rq_ref.at[0, 0, :, wide]
        elif item == PARTS:
            source, target = k_out.at[ctx], rk_ref.at[0, 0, :, narrow]
        else:
            source, target = v_out.at[ctx], rv_ref.at[0, 0, :, narrow]
        return pltpu.make_async_remote_copy(
            src_ref=source,
            dst_ref=target,
            send_sem=out_send.at[ctx, item],
            recv_sem=out_recv.at[slot, item],
            device_id=before_device(ctx),
            device_id_type=MESH,
        )

    def sum_copy(place, slot):
        return pltpu.make_async_remote_copy(
            src_ref=sums.at[my_place],
            dst_ref=sums.at[slot],
            send_sem=sum_send.at[place],
            recv_sem=sum_recv.at[slot],
            device_id=place_device(place),
            device_id_type=MESH,
        )

    o_copy = pltpu.make_async_copy(o_ref.at[0, 0], o_own, local_sem.at[4])
    g_copy = pltpu.make_async_copy(g_ref.at[0, 0], g_own, local_sem.at[5])

    small_copies = [
        pltpu.make_async_copy(source, target, local_sem.at[6 + item])
        for item, (source, target) in enumerate(
            ((lse_far, lse_ref), (bq_far, bq_ref), (bk_far, bk_ref), (bv_far, bv_ref))
        )
    ]

    barrier = pltpu.get_barrier_semaphore()
    for step in range(1, everyone):
        pl.semaphore_signal(
            barrier,
            inc=1,
            device_id=place_device((my_place + step) % everyone),
            device_id_type=MESH,
        )

    @pl.when(has_before)
    def _():
        for ctx in range(n_ctx):
            pl.semaphore_signal(barrier, inc=1, device_id=before_device(ctx), device_id_type=MESH)

    @pl.when(has_after)
    def _():
        for ctx in range(n_ctx):
            pl.semaphore_signal(barrier, inc=1, device_id=after_device(ctx), device_id_type=MESH)

    o_copy.start()
    g_copy.start()
    for copy in small_copies:
        copy.start()
    own_items = [item for item in range(in_items) if item != 2]
    for item in own_items:
        own_copy(item).start()
    bias[:, :GROUP_WIDTH] = jnp.zeros((8, GROUP_WIDTH), jnp.float32)

    neighbours = jnp.where(has_before, n_ctx, 0) + jnp.where(has_after, n_ctx, 0)
    pl.semaphore_wait(barrier, everyone - 1 + neighbours)

    def send(items):
        for step in reversed(range(1, n_ctx)):
            for item in items:
                in_copy(item, partner(me, step, n_ctx), me).start()

    send((0, 1))
    send((3, 4))

    o_copy.wait()
    g_copy.wait()
    for copy in small_copies:
        copy.wait()
    for group in range(KEY_VALUE_HEADS):
        lines = [lse_ref[0, 0, pl.ds(group * GROUP, GROUP), :]]
        for head in range(group * GROUP, (group + 1) * GROUP):
            columns = slice(head * HEAD_SIZE, (head + 1) * HEAD_SIZE)
            product = g_own[:, columns].astype(jnp.float32) * o_own[:, columns].astype(jnp.float32)
            lines.append(jnp.sum(product.T, axis=0, keepdims=True))
        rows_out[group] = jnp.concatenate(lines, axis=0)
    send((2,))
    for part in range(1, PARTS):
        send((3 + 2 * part, 4 + 2 * part))
    rows_in[me] = rows_out[me]

    for ctx in range(n_ctx):
        wide = slice(ctx * GROUP_WIDTH, (ctx + 1) * GROUP_WIDTH)
        narrow = slice(ctx * HEAD_SIZE, (ctx + 1) * HEAD_SIZE)

        @pl.when(me == ctx)
        def _():
            bias[0:1, :] = bq_ref[:, wide].astype(jnp.float32)
            bias[1:2, :HEAD_SIZE] = bk_ref[:, narrow].astype(jnp.float32)
            bias[2:3, :HEAD_SIZE] = bv_ref[:, narrow].astype(jnp.float32)

    for item in own_items:
        own_copy(item).wait()
    for step in range(1, n_ctx):
        for item in (0, 1):
            in_copy(item, partner(me, step, n_ctx), partner(me, step, n_ctx)).wait_recv()
    for ctx in range(n_ctx):
        k_low = (k_in[ctx].astype(jnp.float32) + bias[1:2, :HEAD_SIZE]).astype(jnp.bfloat16)
        k_all[ctx] = k_low
        k_turned[ctx] = k_low.astype(jnp.float32).T.astype(jnp.bfloat16)
        v_all[ctx] = (v_in[ctx].astype(jnp.float32) + bias[2:3, :HEAD_SIZE]).astype(jnp.bfloat16)
    grad_k[...] = jnp.zeros_like(grad_k)
    grad_v[...] = jnp.zeros_like(grad_v)

    def positions(block, local):
        late = (2 * n_ctx - 1 - block) * half + local - half
        return jnp.where(local < half, block * half + local, late)

    q_local = jnp.concatenate(
        [lax.broadcasted_iota(jnp.int32, (1, tokens), 1)] * PART_HEADS, axis=1
    )
    k_local = lax.broadcasted_iota(jnp.int32, (tokens, 1), 0)
    head_sums = [jnp.zeros((1, HEAD_SIZE), jnp.float32) for _ in range(GROUP)]

    order = [(part, 0) for part in range(PARTS)]
    order += [(part, step) for part in range(PARTS) for step in range(1, n_ctx)]
    for part, step in order:
        block = partner(me, step, n_ctx)
        if step:
            for item in ((2,) if part == 0 else ()) + (3 + 2 * part, 4 + 2 * part):
                in_copy(item, block, block).wait_recv()
        for head in range(PART_HEADS):
            columns = slice(head * HEAD_SIZE, (head + 1) * HEAD_SIZE)
            wide = slice(
                part * PART_WIDTH + head * HEAD_SIZE, part * PART_WIDTH + (head + 1) * HEAD_SIZE
            )
            rows = slice(head * tokens, (head + 1) * tokens)
            q_stack[rows] = (
                q_in[block, part, :, columns].astype(jnp.float32) + bias[0:1, wide]
            ).astype(jnp.bfloat16)
            g_stack[rows] = g_in[block, part, :, columns]
        grad_q_turned[...] = jnp.zeros_like(grad_q_turned)
        lines = rows_in[block]
        heads = range(part * PART_HEADS, (part + 1) * PART_HEADS)
        lse_line = jnp.concatenate([lines[h : h + 1] for h in heads], axis=1)
        delta_line = jnp.concatenate([lines[GROUP + h : GROUP + h + 1] for h in heads], axis=1)
        q_pos = positions(block, q_local)

        def over_keys(owner, _):
            queries, gradients = q_stack[...], g_stack[...]
            scores = lax.dot_general(
                k_all[owner], queries, NT, preferred_element_type=jnp.float32
            )
            causal = positions(owner, k_local) <= q_pos
            prob = jnp.where(causal, jnp.exp(scores * scale - lse_line), 0.0)
            grad_prob = lax.dot_general(
                v_all[owner], gradients, NT, preferred_element_type=jnp.float32
            )
            score_low = (prob * (grad_prob - delta_line)).astype(jnp.bfloat16)
            prob_low = prob.astype(jnp.bfloat16)
            grad_v[owner] += lax.dot_general(
                prob_low, gradients, NN, preferred_element_type=jnp.float32
            )
            grad_k[owner] += lax.dot_general(
                score_low, queries, NN, preferred_element_type=jnp.float32
            )
            grad_q_turned[...] += lax.dot_general(
                k_turned[owner], score_low, NN, preferred_element_type=jnp.float32
            )
            return 0

        lax.fori_loop(0, n_ctx, over_keys, 0)
        for head in range(PART_HEADS):
            columns = slice(head * HEAD_SIZE, (head + 1) * HEAD_SIZE)
            grad_q = grad_q_turned[:, head * tokens : (head + 1) * tokens].T * scale
            head_sums[part * PART_HEADS + head] += jnp.sum(grad_q, axis=0, keepdims=True)
            q_out[block, part, :, columns] = grad_q.astype(jnp.bfloat16)

        @pl.when(has_before)
        def _():
            out_copy(part, block, me).start()

    key_sum = jnp.zeros((1, HEAD_SIZE), jnp.float32)
    value_sum = jnp.zeros((1, HEAD_SIZE), jnp.float32)
    for ctx in range(n_ctx):
        key_part = grad_k[ctx] * scale
        k_out[ctx] = key_part.astype(jnp.bfloat16)
        v_out[ctx] = grad_v[ctx].astype(jnp.bfloat16)
        key_sum += jnp.sum(key_part, axis=0, keepdims=True)
        value_sum += jnp.sum(grad_v[ctx], axis=0, keepdims=True)
    blank = jnp.zeros((8 - GROUP - 2, HEAD_SIZE), jnp.float32)
    sums[my_place] = jnp.concatenate(head_sums + [key_sum, value_sum, blank], axis=0)
    for step in range(1, everyone):
        place = (my_place + step) % everyone
        sum_copy(place, my_place).start()

    @pl.when(has_before)
    def _():
        for step in reversed(range(n_ctx)):
            for item in range(PARTS, out_items):
                out_copy(item, partner(me, step, n_ctx), me).start()

    @pl.when(section == n_section - 1)
    def _():
        o_own[...] = jnp.zeros_like(o_own)
        blanks = [
            pltpu.make_async_copy(o_own, rq_ref.at[0, 0], local_sem.at[0]),
            pltpu.make_async_copy(
                o_own.at[:, : KEY_VALUE_HEADS * HEAD_SIZE], rk_ref.at[0, 0], local_sem.at[1]
            ),
            pltpu.make_async_copy(
                o_own.at[:, : KEY_VALUE_HEADS * HEAD_SIZE], rv_ref.at[0, 0], local_sem.at[2]
            ),
        ]
        for copy in blanks:
            copy.start()
        for copy in blanks:
            copy.wait()

    for step in range(1, everyone):
        place = (my_place + step) % everyone
        sum_copy(place, place).wait_recv()
    for ctx in range(n_ctx):
        total = sums[ctx]
        for other in range(1, n_dp):
            total += sums[other * n_ctx + ctx]
        for head in range(GROUP):
            start = ctx * GROUP_WIDTH + head * HEAD_SIZE
            sum_q_ref[:, start : start + HEAD_SIZE] = total[head : head + 1]
        narrow = slice(ctx * HEAD_SIZE, (ctx + 1) * HEAD_SIZE)
        sum_k_ref[:, narrow] = total[GROUP : GROUP + 1]
        sum_v_ref[:, narrow] = total[GROUP + 1 : GROUP + 2]

    for step in range(1, n_ctx):
        for item in range(in_items):
            in_copy(item, partner(me, step, n_ctx), me).wait_send()
    for step in range(1, everyone):
        sum_copy((my_place + step) % everyone, my_place).wait_send()

    @pl.when(has_before)
    def _():
        for ctx in range(n_ctx):
            for item in range(out_items):
                out_copy(item, ctx, me).wait_send()

    @pl.when(has_after)
    def _():
        for ctx in range(n_ctx):
            for item in range(out_items):
                out_copy(item, ctx, ctx).wait_recv()


def placing(*refs):
    sources, targets, held, sems = refs[:6], refs[6:12], refs[12:18], refs[18]
    fetches = [
        pltpu.make_async_copy(source, slot, sems.at[0, item])
        for item, (source, slot) in enumerate(zip(sources, held))
    ]
    stores = [
        pltpu.make_async_copy(slot, target, sems.at[1, item])
        for item, (slot, target) in enumerate(zip(held, targets))
    ]
    for copy in fetches:
        copy.start()
    for fetch, store in zip(fetches, stores):
        fetch.wait()
        store.start()
    for copy in stores:
        copy.wait()


def solution(mesh):
    n_section, n_ctx, n_dp = mesh.shape["section"], mesh.shape["ctx"], mesh.shape["dp"]
    assert n_ctx == KEY_VALUE_HEADS

    def body(q_in, key_in, value_in, out_saved, out_grad, lse, bias_q, key_bias, value_bias):
        tokens = q_in.shape[2]
        width_q, width_k = QUERY_HEADS * HEAD_SIZE, KEY_VALUE_HEADS * HEAD_SIZE
        everyone = n_ctx * n_dp
        anywhere = pl.BlockSpec(memory_space=pl.ANY)
        vmem = pl.BlockSpec(memory_space=pltpu.VMEM)
        hbm = pl.BlockSpec(memory_space=pltpu.HBM)
        low, full = jnp.bfloat16, jnp.float32
        results = pl.pallas_call(
            functools.partial(kernel, n_section, n_ctx, n_dp),
            out_shape=(
                jax.ShapeDtypeStruct((1, 1, tokens, width_q), low),
                jax.ShapeDtypeStruct((1, 1, tokens, width_k), low),
                jax.ShapeDtypeStruct((1, 1, tokens, width_k), low),
                jax.ShapeDtypeStruct((1, width_q), full),
                jax.ShapeDtypeStruct((1, width_k), full),
                jax.ShapeDtypeStruct((1, width_k), full),
            ),
            in_specs=[hbm] * 9,
            out_specs=(anywhere, anywhere, anywhere, vmem, vmem, vmem),
            scratch_shapes=[
                pltpu.VMEM((n_ctx, PARTS, tokens, PART_WIDTH), low),
                pltpu.VMEM((n_ctx, PARTS, tokens, PART_WIDTH), low),
                pltpu.VMEM((n_ctx, tokens, HEAD_SIZE), low),
                pltpu.VMEM((n_ctx, tokens, HEAD_SIZE), low),
                pltpu.VMEM((n_ctx, 2 * GROUP, tokens), full),
                pltpu.VMEM((n_ctx, 2 * GROUP, tokens), full),
                pltpu.VMEM((tokens, width_q), low),
                pltpu.VMEM((tokens, width_q), low),
                pltpu.VMEM((8, GROUP_WIDTH), full),
                pltpu.VMEM((n_ctx, tokens, HEAD_SIZE), low),
                pltpu.VMEM((n_ctx, tokens, HEAD_SIZE), low),
                pltpu.VMEM((n_ctx, HEAD_SIZE, tokens), low),
                pltpu.VMEM((n_ctx, tokens, HEAD_SIZE), full),
                pltpu.VMEM((n_ctx, tokens, HEAD_SIZE), full),
                pltpu.VMEM((HEAD_SIZE, PART_HEADS * tokens), full),
                pltpu.VMEM((PART_HEADS * tokens, HEAD_SIZE), low),
                pltpu.VMEM((PART_HEADS * tokens, HEAD_SIZE), low),
                pltpu.VMEM((n_ctx, PARTS, tokens, PART_WIDTH), low),
                pltpu.VMEM((n_ctx, tokens, HEAD_SIZE), low),
                pltpu.VMEM((n_ctx, tokens, HEAD_SIZE), low),
                pltpu.VMEM((everyone, 8, HEAD_SIZE), full),
                pltpu.SemaphoreType.DMA((n_ctx, 3 + 2 * PARTS)),
                pltpu.SemaphoreType.DMA((n_ctx, 3 + 2 * PARTS)),
                pltpu.SemaphoreType.DMA((n_ctx, PARTS + 2)),
                pltpu.SemaphoreType.DMA((n_ctx, PARTS + 2)),
                pltpu.SemaphoreType.DMA((everyone,)),
                pltpu.SemaphoreType.DMA((everyone,)),
                pltpu.SemaphoreType.DMA((3 + 2 * PARTS,)),
                pltpu.SemaphoreType.DMA((10,)),
                pltpu.VMEM(lse.shape, full),
                pltpu.VMEM(bias_q.shape, low),
                pltpu.VMEM(key_bias.shape, low),
                pltpu.VMEM(value_bias.shape, low),
            ],
            compiler_params=pltpu.CompilerParams(
                collective_id=0, has_side_effects=True, vmem_limit_bytes=64 * 1024 * 1024
            ),
        )(q_in, key_in, value_in, out_saved, out_grad, lse, bias_q, key_bias, value_bias)
        return pl.pallas_call(
            placing,
            out_shape=tuple(jax.ShapeDtypeStruct(r.shape, r.dtype) for r in results),
            in_specs=[anywhere] * 6,
            out_specs=(hbm,) * 6,
            scratch_shapes=[pltpu.VMEM(r.shape, r.dtype) for r in results]
            + [pltpu.SemaphoreType.DMA((2, 6))],
            compiler_params=pltpu.CompilerParams(vmem_limit_bytes=64 * 1024 * 1024),
        )(*results)

    rows = P("dp", "section", "ctx", None)
    line = P("section", None)
    return jax.shard_map(
        body,
        mesh=mesh,
        in_specs=(rows,) * 5 + (P("dp", "section", None, "ctx"),) + (line,) * 3,
        out_specs=(rows,) * 3 + (line,) * 3,
        check_vma=False,
    )
```
